32 devices in a mesh: front: 2 (over y), row: 2 (over x), col: 8 (over z, core).
Axes of the slice: x: 2, y: 2, z: 4, core: 2. Of those that a mesh axis runs over, the one named last changes fastest.
Arguments:
- front_orig: bfloat16 [2, 12288, 12288], P('front', 'row', 'col'), as said below
- child_update: bfloat16 [8192, 32768], P(('front', 'row'), 'col'), as said below
- tile_map: int32 [2, 2, 64], replicated, may hold values from 0 to 95, as said below
Outputs:
- update: float32 [2, 12288, 12288], P('front', 'row', 'col')
- factor: float32 [2, 12288, 512], P('front', 'row')
The draws below stay inside these ranges and needn't reach their ends.
Inputs may be any that keep to these rules, and one draw needn't show every extreme that they name: For every f and c, tile_map[f, c] is one-to-one. tile_map[f, c, i] mod 8 depends only on i mod 8 and takes each of its 8 values once over 8 consecutive i; tile_map[f, c, i] mod 2 depends only on i mod 2. `front_orig`: each front is symmetric in logical order. `child_update`: each child's 8192 x 8192 matrix is symmetric.
All inputs are finite; a program needn't handle non-finite values.
Results may differ from the reference program's by a relative error of at most 0.0009.
Values may be sent and summed in bfloat16 or wider, within the bound.
A program may use at most 192 MiB of HBM per device.

```python
import math
import jax
import jax.numpy as jnp
from jax import lax

TILE = 128
NF = 12288
NC = 8192
PANELS = 2
PANEL = 256
NT = 96
NCT = 64
N_ROW = 2
N_COL = 8


def symmetric_noise(key, count, order):
    raw_draw = jax.random.normal(key, (count, order, order), jnp.float32)
    return (raw_draw + jnp.swapaxes(raw_draw, 1, 2)) * 0.70710678


def to_storage(matrix):
    shaped = matrix.reshape(2, NT // N_ROW, N_ROW, TILE, NF).transpose(0, 2, 1, 3, 4).reshape(2, NF, NF)
    shaped = shaped.reshape(2, NF, NT // N_COL, N_COL, TILE).transpose(0, 1, 3, 2, 4).reshape(2, NF, NF)
    return shaped


def draw_front_orig(key, part):
    key_noise, key_diag, key_rank = jax.random.split(key, 3)
    matrix = symmetric_noise(key_noise, 2, NF) * (0.25 / math.sqrt(NF))
    diag_vals = jax.random.uniform(key_diag, (2, NF), jnp.float32, 2.5, 3.5)
    factor_vals = jax.random.normal(key_rank, (4, 2, NF), jnp.float32) * 0.125
    for factor_no in range(4):
        matrix = matrix + factor_vals[factor_no][:, :, None] * factor_vals[factor_no][:, None, :]
    identity = jnp.eye(NF, dtype=jnp.float32)
    matrix = matrix + diag_vals[:, :, None] * identity[None]
    return to_storage(matrix).astype(jnp.bfloat16)


def draw_child_update(key, part):
    key_noise, key_diag = jax.random.split(key, 2)
    matrix = symmetric_noise(key_noise, 4, NC) * (0.25 / math.sqrt(NC))
    shrink = jax.random.uniform(key_diag, (4, NC), jnp.float32, 0.125, 0.375)
    identity = jnp.eye(NC, dtype=jnp.float32)
    matrix = matrix - shrink[:, :, None] * identity[None]
    return matrix.transpose(1, 0, 2).reshape(NC, 4 * NC).astype(jnp.bfloat16)


def pick_quotients(key):
    per_class = NCT // N_COL
    quotients = NT // N_COL
    key_mid, key_order = jax.random.split(key, 2)
    middle = 1 + jax.random.permutation(key_mid, quotients - 2)[:per_class - 2]
    chosen = jnp.concatenate([jnp.array([0, quotients - 1], dtype=jnp.int32), middle.astype(jnp.int32)])
    return chosen[jax.random.permutation(key_order, per_class)]


def one_map(key):
    key_rho, key_high, key_quot = jax.random.split(key, 3)
    rho_perm = jax.random.permutation(key_rho, N_ROW).astype(jnp.int32)
    high_perm = jax.random.permutation(key_high, N_COL // N_ROW).astype(jnp.int32)
    residue_ids = jnp.arange(N_COL)
    residues = rho_perm[residue_ids % N_ROW] + N_ROW * high_perm[residue_ids // N_ROW]
    quot_table = jax.vmap(pick_quotients)(jax.random.split(key_quot, N_COL))
    child_ids = jnp.arange(NCT)
    return N_COL * quot_table[child_ids % N_COL, child_ids // N_COL] + residues[child_ids % N_COL]


def draw_tile_map(key, part):
    key_list = jax.random.split(jax.random.fold_in(key, 7), 4)
    return jax.vmap(one_map)(key_list).reshape(2, 2, NCT).astype(jnp.int32)


def setup_inputs(seed: int = 0) -> dict:
    splits = jax.random.split(jax.random.key(seed), 4)
    front_orig = draw_front_orig(jax.random.fold_in(splits[3], 71), 0)
    child_update = draw_child_update(jax.random.fold_in(splits[3], 71), 0)
    tile_map = draw_tile_map(jax.random.fold_in(splits[3], 71), 0)
    return dict(front_orig=front_orig, child_update=child_update, tile_map=tile_map)


def reorder_rows(matrix, groups, forward):
    per_group = matrix.shape[0] // TILE // groups
    if forward:
        shaped = matrix.reshape(groups, per_group, TILE, matrix.shape[1])
    else:
        shaped = matrix.reshape(per_group, groups, TILE, matrix.shape[1])
    return shaped.transpose(1, 0, 2, 3).reshape(matrix.shape)

def reference(front_orig, child_update, tile_map):
    identity = jnp.eye(PANEL, dtype=jnp.float32)
    row_index = jnp.arange(NF)
    updates = []
    factors = []
    for parent in range(2):
        front_mat = front_orig[parent].astype(jnp.float32)
        front_mat = reorder_rows(front_mat, N_ROW, True)
        front_mat = reorder_rows(front_mat.T, N_COL, True).T
        tile_grid = front_mat.reshape(NT, TILE, NT, TILE).transpose(0, 2, 1, 3)
        for sibling in range(2):
            column_start = (2 * parent + sibling) * NC
            child_mat = child_update[:, column_start:column_start + NC].astype(jnp.float32)
            child_grid = child_mat.reshape(NCT, TILE, NCT, TILE).transpose(0, 2, 1, 3)
            mapped = tile_map[parent, sibling]
            tile_grid = tile_grid.at[mapped[:, None], mapped[None, :]].add(child_grid)
        front_mat = tile_grid.transpose(0, 2, 1, 3).reshape(NF, NF)
        columns = []
        for panel_no in range(PANELS):
            start_col = panel_no * PANEL
            stop_col = start_col + PANEL
            lower_f = jnp.linalg.cholesky(front_mat[start_col:stop_col, start_col:stop_col])
            inverse = jax.scipy.linalg.solve_triangular(lower_f, identity, lower=True)
            panel_cols = jnp.dot(front_mat[:, start_col:stop_col].astype(jnp.float32), inverse.T.astype(jnp.float32), precision=lax.Precision.HIGHEST, preferred_element_type=jnp.float32)
            panel_cols = jnp.where((row_index >= start_col)[:, None], panel_cols, 0.0)
            columns.append(panel_cols)
            trail_rows = jnp.where((row_index >= stop_col)[:, None], panel_cols, 0.0)
            front_mat = front_mat - jnp.dot(trail_rows.astype(jnp.float32), trail_rows.T.astype(jnp.float32), precision=lax.Precision.HIGHEST, preferred_element_type=jnp.float32)
        front_mat = reorder_rows(front_mat, N_ROW, False)
        front_mat = reorder_rows(front_mat.T, N_COL, False).T
        updates.append(front_mat)
        factors.append(reorder_rows(jnp.concatenate(columns, axis=1), N_ROW, False))
    return (jnp.stack(updates), jnp.stack(factors))
```

```python
import functools

import jax
import jax.numpy as jnp
from jax import lax
from jax.experimental import pallas as pl
from jax.experimental.pallas import tpu as pltpu
from jax.sharding import PartitionSpec as P

TILE = 128
PANELS = 2
PANEL = 256
KT = PANELS * PANEL // TILE
KW = KT * TILE
HI = lax.Precision.HIGHEST
MESH = pl.DeviceIdType.MESH


def pack_kernel(row_count, col_count, cap_cols, group, rows_ref, cols_ref, in_ref, out_ref):
    step = pl.program_id(0)
    for dest_row in range(row_count):
        row = rows_ref[dest_row, step]
        row = pl.multiple_of(row * TILE, TILE)
        for dest_col in range(col_count):
            for slot in range(cap_cols):
                col = pl.multiple_of(cols_ref[dest_col * cap_cols + slot] * TILE, TILE)
                out_ref[dest_row * col_count + dest_col, 0, slot] = in_ref[
                    pl.ds(row, TILE), pl.ds(col, TILE)
                ]


def pack(child, rows, cols, row_count, col_count, cap_rows, cap_cols):
    peers = row_count * col_count
    width = child.shape[1]
    body = functools.partial(pack_kernel, row_count, col_count, cap_cols, 1)

    def wrapped(rows_ref, cols_ref, *refs):
        ins, out_ref = refs[:-1], refs[-1]
        for dest_row in range(row_count):
            for dest_col in range(col_count):
                for slot in range(cap_cols):
                    col = pl.multiple_of(cols_ref[dest_col * cap_cols + slot] * TILE, TILE)
                    out_ref[dest_row * col_count + dest_col, 0, slot] = ins[dest_row][
                        :, pl.ds(col, TILE)
                    ]

    def row_map(dest_row, step, rows_ref, cols_ref):
        return (rows_ref[dest_row, step], 0)

    del body
    return pl.pallas_call(
        wrapped,
        grid_spec=pltpu.PrefetchScalarGridSpec(
            num_scalar_prefetch=2,
            grid=(cap_rows,),
            in_specs=[
                pl.BlockSpec((TILE, width), functools.partial(row_map, dest_row))
                for dest_row in range(row_count)
            ],
            out_specs=pl.BlockSpec(
                (peers, 1, cap_cols, TILE, TILE), lambda step, *_: (0, step, 0, 0, 0)
            ),
        ),
        out_shape=jax.ShapeDtypeStruct((peers, cap_rows, cap_cols, TILE, TILE), child.dtype),
        compiler_params=pltpu.CompilerParams(vmem_limit_bytes=40 * 2**20),
        name="pack_tiles",
    )(rows, cols, *([child] * row_count))


def exchange_kernel(sizes, low, count, has_prior, *refs):
    row_count, col_count, half = sizes
    out_ref = refs[0]
    recv_ref, stage_ref, send_sem, recv_sem, pass_send, pass_recv, own_sem = refs[-7:]
    peers = row_count * col_count
    front = lax.axis_index("front")
    row = lax.axis_index("row")
    col = lax.axis_index("col")
    me = row * col_count + col
    kept = (col // half) == front
    slot = row * half + col % half
    part = pl.ds(low, count)

    barrier = pltpu.get_barrier_semaphore()

    def greet(off, carry):
        dest = (me + off) % peers
        pl.semaphore_signal(
            barrier, inc=1, device_id=(front, dest // col_count, dest % col_count),
            device_id_type=MESH,
        )
        return carry

    lax.fori_loop(1, peers, greet, 0)
    pl.semaphore_signal(barrier, inc=1, device_id=(1 - front, row, col), device_id_type=MESH)
    pl.semaphore_wait(barrier, peers)

    def send(off, target):
        dest = (me + off) % peers
        return pltpu.make_async_remote_copy(
            src_ref=out_ref.at[dest, part],
            dst_ref=target,
            send_sem=send_sem.at[off],
            recv_sem=recv_sem.at[off],
            device_id=(front, dest // col_count, dest % col_count),
            device_id_type=MESH,
        )

    def forward(source, where):
        return pltpu.make_async_remote_copy(
            src_ref=source,
            dst_ref=recv_ref.at[1, where, part],
            send_sem=pass_send.at[where],
            recv_sem=pass_recv.at[where],
            device_id=(1 - front, row, col),
            device_id_type=MESH,
        )

    own = pltpu.make_async_copy(out_ref.at[me, part], recv_ref.at[0, slot, part], own_sem)

    @pl.when(kept)
    def _():
        def start(off, carry):
            send(off, recv_ref.at[0, slot, part]).start()
            return carry

        lax.fori_loop(1, peers, start, 0)
        own.start()

    @pl.when(jnp.logical_not(kept))
    def _():
        def start(off, carry):
            send(off, stage_ref.at[slot]).start()
            return carry

        lax.fori_loop(1, peers, start, 0)
        forward(out_ref.at[me, part], slot).start()

    def relay(off, carry):
        source = (me + peers - off) % peers
        source_col = source % col_count
        where = (source // col_count) * half + source_col % half

        @pl.when((source_col // half) != front)
        def _():
            send(off, stage_ref.at[where]).wait_recv()
            forward(stage_ref.at[where], where).start()

        return carry

    lax.fori_loop(1, peers, relay, 0)

    def finish(off, carry):
        source = (me + peers - off) % peers
        source_col = source % col_count
        where = (source // col_count) * half + source_col % half

        @pl.when((source_col // half) == front)
        def _():
            send(off, recv_ref.at[0, where, part]).wait_recv()

        send(off, stage_ref.at[slot]).wait_send()
        return carry

    lax.fori_loop(1, peers, finish, 0)

    @pl.when(kept)
    def _():
        own.wait()

    def close(where, carry):
        forward(stage_ref.at[where], where).wait_send()
        forward(stage_ref.at[where], where).wait_recv()
        return carry

    lax.fori_loop(0, row_count * half, close, 0)


def exchange(outgoing, prior, token, sizes, low, count, number):
    row_count, col_count, half = sizes
    peers = row_count * col_count
    slots = row_count * half
    cap_rows, cap_cols = outgoing.shape[1:3]
    anywhere = pl.BlockSpec(memory_space=pl.ANY)
    operands = [outgoing]
    aliases = {}
    if prior is not None:
        operands += [token, prior]
        aliases = {2: 0}
    recv, _ = pl.pallas_call(
        functools.partial(exchange_kernel, sizes, low, count, prior is not None),
        out_shape=(
            jax.ShapeDtypeStruct((2, slots, cap_rows, cap_cols, TILE, TILE), outgoing.dtype),
            jax.ShapeDtypeStruct((slots, count, cap_cols, TILE, TILE), outgoing.dtype),
        ),
        in_specs=[anywhere] * len(operands),
        out_specs=(anywhere, anywhere),
        scratch_shapes=[
            pltpu.SemaphoreType.DMA((peers,)),
            pltpu.SemaphoreType.DMA((peers,)),
            pltpu.SemaphoreType.DMA((slots,)),
            pltpu.SemaphoreType.DMA((slots,)),
            pltpu.SemaphoreType.DMA,
        ],
        input_output_aliases=aliases,
        compiler_params=pltpu.CompilerParams(collective_id=number, has_side_effects=True),
        name="exchange_tiles_%d" % number,
    )(*operands)
    return recv


def combine_kernel(rows_at, local_ct, cap_cols, update, place_ref, cols_ref, *refs):
    step = pl.program_id(0)
    tiles = refs[: 2 * rows_at]
    front_ref = refs[2 * rows_at]
    out_ref = refs[-1]
    for at in range(rows_at):
        span = pl.ds(at * TILE, TILE)
        for ct in range(local_ct):
            lanes = pl.ds(ct * TILE, TILE)
            total = front_ref[0, span, lanes].astype(jnp.float32)
            for sib in range(2):
                where = cols_ref[sib, ct]
                there = (place_ref[3, sib, step * rows_at + at] > 0) & (where >= 0)
                where = jnp.maximum(where, 0)
                tile = tiles[2 * at + sib][0, where // cap_cols, 0, where % cap_cols]
                total = total + jnp.where(there, tile.astype(jnp.float32), 0.0)
            out_ref[0, span, lanes] = total
    if update:
        left_ref, right_ref = refs[2 * rows_at + 1 : 2 * rows_at + 3]
        for ct in range(0, local_ct, 2):
            lanes = pl.ds(ct * TILE, 2 * TILE)
            out_ref[0, :, lanes] -= lax.dot_general(
                left_ref[...], right_ref[:, lanes], (((1,), (0,)), ((), ())),
                preferred_element_type=jnp.float32,
            )


def combine(recv, front_block, place, cols, sizes, row_tiles, rows_at, factors):
    row_count, col_count, half = sizes
    quarter = half // 2
    cap_rows, cap_cols = recv.shape[2:4]
    width = front_block.shape[2]
    local_ct = width // TILE

    def tile_map(at, sib, step, place_ref, cols_ref):
        tile = step * rows_at + at
        return (place_ref[0, sib, tile], place_ref[1, sib, tile], place_ref[2, sib, tile], 0, 0, 0)

    recv = recv.reshape(2, row_count * 2, quarter, cap_rows, cap_cols, TILE, TILE)
    recv = recv.reshape(4 * row_count, quarter, cap_rows, cap_cols, TILE, TILE)

    def block_map(at, sib, step, place_ref, cols_ref):
        tile = step * rows_at + at
        return (place_ref[0, sib, tile], 0, place_ref[1, sib, tile], 0, 0, 0)

    in_specs = []
    for at in range(rows_at):
        for sib in range(2):
            in_specs.append(
                pl.BlockSpec(
                    (1, quarter, 1, cap_cols, TILE, TILE), functools.partial(block_map, at, sib)
                )
            )
    in_specs.append(pl.BlockSpec((1, rows_at * TILE, width), lambda step, *_: (0, step, 0)))
    operands = [recv] * (2 * rows_at) + [front_block]
    if factors is not None:
        in_specs.append(pl.BlockSpec((rows_at * TILE, KW), lambda step, *_: (step, 0)))
        in_specs.append(pl.BlockSpec((KW, width), lambda step, *_: (0, 0)))
        operands += list(factors)
    return pl.pallas_call(
        functools.partial(combine_kernel, rows_at, local_ct, cap_cols, factors is not None),
        grid_spec=pltpu.PrefetchScalarGridSpec(
            num_scalar_prefetch=2,
            grid=(row_tiles // rows_at,),
            in_specs=in_specs,
            out_specs=pl.BlockSpec((1, rows_at * TILE, width), lambda step, *_: (0, step, 0)),
        ),
        out_shape=jax.ShapeDtypeStruct((1, row_tiles * TILE, width), jnp.float32),
        compiler_params=pltpu.CompilerParams(vmem_limit_bytes=48 * 2**20),
        name="combine_update" if factors is not None else "combine_pivot_rows",
    )(place, cols, *operands)


def per_device(front_orig, child_update, tile_map):
    row_count = lax.axis_size("row")
    col_count = lax.axis_size("col")
    front_id = lax.axis_index("front")
    row_id = lax.axis_index("row")
    col_id = lax.axis_index("col")
    local_rt = front_orig.shape[1] // TILE
    local_ct = front_orig.shape[2] // TILE
    band_rows = child_update.shape[0] // TILE
    band_cols = child_update.shape[1] // TILE
    nct = tile_map.shape[2]
    cap_rows = max(1, band_rows // row_count)
    cap_cols = max(1, band_cols // col_count)
    half = col_count // 2
    quarter = col_count // 4
    ratio = col_count // row_count
    sizes = (row_count, col_count, half)
    pivot_tiles = max(1, KT // row_count)

    every = jnp.arange(nct)
    band_of = every // band_rows
    same = (band_of[:, None] == band_of[None, :]) & (
        tile_map[..., :, None] % row_count == tile_map[..., None, :] % row_count
    )
    before = same & (tile_map[..., None, :] < tile_map[..., :, None])
    rank = jnp.sum(before.astype(jnp.int32), axis=-1)

    child_no = col_id // quarter
    sender_map = tile_map[child_no // 2, child_no % 2]
    sender_rank = rank[child_no // 2, child_no % 2]
    first = (front_id * row_count + row_id) * band_rows
    band_map = lax.dynamic_slice(sender_map, (first,), (band_rows,))
    band_rank = lax.dynamic_slice(sender_rank, (first,), (band_rows,))
    wanted = jnp.arange(row_count * cap_rows)[:, None]
    rows = jnp.sum(
        jnp.where(
            (band_map % row_count * cap_rows + band_rank)[None, :] == wanted,
            jnp.arange(band_rows)[None, :],
            0,
        ),
        axis=1,
    ).reshape(row_count, cap_rows)
    col_map = lax.dynamic_slice(sender_map, (col_id % quarter * band_cols,), (band_cols,))
    wanted = jnp.arange(col_count * cap_cols)[:, None]
    cols = jnp.sum(
        jnp.where(
            (col_map % col_count * cap_cols + jnp.arange(band_cols) // col_count)[None, :]
            == wanted,
            jnp.arange(band_cols)[None, :],
            0,
        ),
        axis=1,
    )
    outgoing = pack(
        child_update, rows.astype(jnp.int32), cols.astype(jnp.int32),
        row_count, col_count, cap_rows, cap_cols,
    )

    own_maps = lax.dynamic_index_in_dim(tile_map, front_id, 0, keepdims=False)
    own_rank = lax.dynamic_index_in_dim(rank, front_id, 0, keepdims=False)
    row_tile = row_id + row_count * jnp.arange(local_rt)
    hit = own_maps[:, None, :] == row_tile[None, :, None]
    source = (every // band_rows)[None, None, :]
    side = jnp.where(source // row_count == front_id, 0, 1)
    sib_no = jnp.arange(2)[:, None, None]
    chunk = (side * row_count + source % row_count) * 2 + sib_no

    def choose(values):
        return jnp.sum(jnp.where(hit, values, 0), axis=-1)

    place = jnp.stack(
        [
            choose(chunk),
            choose(own_rank[:, None, :]),
            jnp.zeros((2, local_rt), jnp.int32),
            choose(1),
        ]
    ).astype(jnp.int32)
    col_tile = col_id + col_count * jnp.arange(local_ct)
    col_hit = own_maps[:, None, :] == col_tile[None, :, None]
    col_place = every // band_cols * cap_cols + every % band_cols // col_count
    col_where = jnp.sum(jnp.where(col_hit, col_place + 1, 0), axis=-1).astype(jnp.int32) - 1

    early = min(pivot_tiles, cap_rows)
    recv = exchange(outgoing, None, None, sizes, 0, early, 1)
    pivot_rows = combine(
        recv, front_orig, place, col_where, sizes, pivot_tiles, 1, None
    )[0]
    gathered = lax.all_gather(pivot_rows.reshape(pivot_tiles, TILE, -1), "row", axis=0)
    gathered = gathered.swapaxes(0, 1).reshape(row_count * pivot_tiles * TILE, -1)[:KW]
    corner = lax.all_gather(gathered[:, :TILE], "col", axis=0)[:KT]
    diagonal = corner.swapaxes(0, 1).reshape(KW, KW)

    if early < cap_rows:
        middle = (cap_rows - early) // 2
        recv = exchange(outgoing, recv, pivot_rows, sizes, early, middle, 2)

    eye = jnp.eye(PANEL, dtype=jnp.float32)
    dot = functools.partial(jnp.dot, precision=HI, preferred_element_type=jnp.float32)
    low0 = jnp.linalg.cholesky(diagonal[:PANEL, :PANEL])
    inv0 = jax.scipy.linalg.solve_triangular(low0, eye, lower=True)
    g10 = dot(diagonal[PANEL:, :PANEL], inv0.T)
    low1 = jnp.linalg.cholesky(diagonal[PANEL:, PANEL:] - dot(g10, g10.T))
    inv1 = jax.scipy.linalg.solve_triangular(low1, eye, lower=True)

    g0 = dot(inv0, gathered[:PANEL])
    g1 = dot(inv1, gathered[PANEL:] - dot(g10, g0))
    col_tiles = jnp.repeat(col_tile, TILE)
    g1 = jnp.where((col_tiles >= 2)[None, :], g1, 0.0)
    mine = jnp.concatenate([g0, g1], axis=0).T
    trail0 = jnp.where((col_tiles >= 2)[None, :], g0, 0.0)
    trail1 = jnp.where((col_tiles >= 4)[None, :], g1, 0.0)
    right = jnp.concatenate([trail0, trail1], axis=0).astype(jnp.bfloat16)

    groups = [[q * row_count + h for h in range(row_count)] for q in range(ratio)]
    share = mine.reshape(row_count, local_ct * TILE // row_count, KW)
    share = lax.all_to_all(
        share, "col", split_axis=0, concat_axis=0, axis_index_groups=groups, tiled=True
    )
    share = lax.dynamic_index_in_dim(share, row_id, 0, keepdims=False)
    whole = lax.all_gather(share, "col", axis=0)

    if early < cap_rows:
        recv = exchange(outgoing, recv, share, sizes, early + middle, cap_rows - early - middle, 3)

    factor = (
        whole.reshape(ratio, local_ct, TILE, KW).swapaxes(0, 1).reshape(local_rt * TILE, KW)
    )
    row_tiles = jnp.repeat(row_tile, TILE)[:, None]
    panel_of = jnp.arange(KW)[None, :] // PANEL
    left = jnp.where(row_tiles >= 2 * panel_of + 2, factor, 0.0).astype(jnp.bfloat16)
    front = combine(recv, front_orig, place, col_where, sizes, local_rt, 2, (left, right))
    return (front, factor[None])


def solution(mesh):
    placed = (P("front", "row", "col"), P(("front", "row"), "col"), P())
    return jax.shard_map(
        per_device,
        mesh=mesh,
        in_specs=placed,
        out_specs=(P("front", "row", "col"), P("front", "row", None)),
        check_vma=False,
    )
```

```python
import functools

import jax
import jax.numpy as jnp
from jax import lax
from jax.experimental import pallas as pl
from jax.experimental.pallas import tpu as pltpu
from jax.sharding import PartitionSpec as P

TILE = 128
PANELS = 2
PANEL = 256
KT = PANELS * PANEL // TILE
KW = KT * TILE
HI = lax.Precision.HIGHEST
MESH = pl.DeviceIdType.MESH


def pack(child, rows, cols, row_count, col_count, cap_rows, cap_cols):
    peers = row_count * col_count
    width = child.shape[1]

    def body(rows_ref, cols_ref, *refs):
        ins, out_ref = refs[:-1], refs[-1]
        for dest_row in range(row_count):
            for dest_col in range(col_count):
                for slot in range(cap_cols):
                    col = pl.multiple_of(cols_ref[dest_col * cap_cols + slot] * TILE, TILE)
                    out_ref[dest_row * col_count + dest_col, 0, slot] = ins[dest_row][
                        :, pl.ds(col, TILE)
                    ]

    def row_map(dest_row, step, rows_ref, cols_ref):
        return (rows_ref[dest_row, step], 0)

    return pl.pallas_call(
        body,
        grid_spec=pltpu.PrefetchScalarGridSpec(
            num_scalar_prefetch=2,
            grid=(cap_rows,),
            in_specs=[
                pl.BlockSpec((TILE, width), functools.partial(row_map, dest_row))
                for dest_row in range(row_count)
            ],
            out_specs=pl.BlockSpec(
                (peers, 1, cap_cols, TILE, TILE), lambda step, *_: (0, step, 0, 0, 0)
            ),
        ),
        out_shape=jax.ShapeDtypeStruct((peers, cap_rows, cap_cols, TILE, TILE), child.dtype),
        compiler_params=pltpu.CompilerParams(vmem_limit_bytes=40 * 2**20),
        name="pack_tiles",
    )(rows, cols, *([child] * row_count))


def invert_factor(diag_ref, inv_ref, work_ref, small_ref, between):
    blocks = KW // TILE
    rows_of = lax.broadcasted_iota(jnp.int32, (KW, KW), 0)
    cols_of = lax.broadcasted_iota(jnp.int32, (KW, KW), 1)
    work_ref[:, :KW] = diag_ref[...]
    work_ref[:, KW:] = jnp.where(rows_of == cols_of, 1.0, 0.0)
    row_no = lax.broadcasted_iota(jnp.int32, (TILE, 1), 0)
    lane_no = lax.broadcasted_iota(jnp.int32, (1, TILE), 1)
    small_rows = lax.broadcasted_iota(jnp.int32, (TILE, TILE), 0)
    small_cols = lax.broadcasted_iota(jnp.int32, (TILE, TILE), 1)
    for block in range(blocks):
        span = pl.ds(block * TILE, TILE)
        small_ref[:, :TILE] = work_ref[span, span]
        small_ref[:, TILE:] = jnp.where(small_rows == small_cols, 1.0, 0.0)

        def step(k, carry):
            pivot_row = small_ref[pl.ds(k, 1), :]
            here = lane_no == k
            pivot = jnp.sum(jnp.where(here, pivot_row[:, :TILE], 0.0), axis=1, keepdims=True)
            scale = 1.0 / jnp.sqrt(pivot)
            column = jnp.sum(jnp.where(here, small_ref[:, :TILE], 0.0), axis=1, keepdims=True)
            scaled = pivot_row * scale
            times = jnp.where(row_no > k, column * scale, 0.0)
            small_ref[...] = jnp.where(row_no == k, scaled, small_ref[...] - times * scaled)
            return carry

        lax.fori_loop(0, TILE, step, 0)
        reduced = jnp.dot(
            small_ref[:, TILE:], work_ref[span, :], precision=HI,
            preferred_element_type=jnp.float32,
        )
        work_ref[span, :] = reduced
        if block + 1 < blocks:
            rest = pl.ds((block + 1) * TILE, KW - (block + 1) * TILE)
            work_ref[rest, :] -= lax.dot_general(
                work_ref[span, rest], work_ref[span, :], (((0,), (0,)), ((), ())),
                precision=HI, preferred_element_type=jnp.float32,
            )
        between(block)
    inv_ref[...] = jnp.where(rows_of >= cols_of, work_ref[:, KW:], 0.0)


def factor_alone(diagonal):
    def body(diag_ref, inv_ref, work_ref, small_ref):
        invert_factor(diag_ref, inv_ref, work_ref, small_ref, lambda block: None)

    return pl.pallas_call(
        body,
        out_shape=jax.ShapeDtypeStruct((KW, KW), jnp.float32),
        scratch_shapes=[
            pltpu.VMEM((KW, 2 * KW), jnp.float32),
            pltpu.VMEM((TILE, 2 * TILE), jnp.float32),
        ],
        compiler_params=pltpu.CompilerParams(vmem_limit_bytes=32 * 2**20),
        name="factor_inverse",
    )(diagonal)


def exchange_kernel(sizes, low, count, inputs, factoring, *refs):
    row_count, col_count, half = sizes
    out_ref = refs[0]
    recv_ref, stage_ref = refs[inputs : inputs + 2]
    if factoring:
        inv_ref, work_ref, small_ref = refs[inputs + 2], refs[-7], refs[-6]
    send_sem, recv_sem, pass_send, pass_recv, own_sem = refs[-5:]
    peers = row_count * col_count
    front = lax.axis_index("front")
    row = lax.axis_index("row")
    col = lax.axis_index("col")
    me = row * col_count + col
    kept = (col // half) == front
    slot = row * half + col % half
    part = pl.ds(low, count)

    barrier = pltpu.get_barrier_semaphore()

    def greet(off, carry):
        dest = (me + off) % peers
        pl.semaphore_signal(
            barrier, inc=1, device_id=(front, dest // col_count, dest % col_count),
            device_id_type=MESH,
        )
        return carry

    lax.fori_loop(1, peers, greet, 0)
    pl.semaphore_signal(barrier, inc=1, device_id=(1 - front, row, col), device_id_type=MESH)
    pl.semaphore_wait(barrier, peers)

    def send(off, target):
        dest = (me + off) % peers
        return pltpu.make_async_remote_copy(
            src_ref=out_ref.at[dest, part],
            dst_ref=target,
            send_sem=send_sem.at[off],
            recv_sem=recv_sem.at[off],
            device_id=(front, dest // col_count, dest % col_count),
            device_id_type=MESH,
        )

    def forward(source, where):
        return pltpu.make_async_remote_copy(
            src_ref=source,
            dst_ref=recv_ref.at[1, where, part],
            send_sem=pass_send.at[where],
            recv_sem=pass_recv.at[where],
            device_id=(1 - front, row, col),
            device_id_type=MESH,
        )

    own = pltpu.make_async_copy(out_ref.at[me, part], recv_ref.at[0, slot, part], own_sem)

    @pl.when(kept)
    def _():
        def start(off, carry):
            send(off, recv_ref.at[0, slot, part]).start()
            return carry

        lax.fori_loop(1, peers, start, 0)
        own.start()

    @pl.when(jnp.logical_not(kept))
    def _():
        def start(off, carry):
            send(off, stage_ref.at[slot]).start()
            return carry

        lax.fori_loop(1, peers, start, 0)
        forward(out_ref.at[me, part], slot).start()

    def relay(off, carry):
        source = (me + peers - off) % peers
        source_col = source % col_count
        where = (source // col_count) * half + source_col % half

        @pl.when((source_col // half) != front)
        def _():
            send(off, stage_ref.at[where]).wait_recv()
            forward(stage_ref.at[where], where).start()

        return carry

    if factoring:
        parts = KW // TILE
        cuts = [1 + (peers - 1) * at // parts for at in range(parts + 1)]

        def between(block):
            lax.fori_loop(cuts[block], cuts[block + 1], relay, 0)

        invert_factor(refs[1], inv_ref, work_ref, small_ref, between)
    else:
        lax.fori_loop(1, peers, relay, 0)

    def finish(off, carry):
        source = (me + peers - off) % peers
        source_col = source % col_count
        where = (source // col_count) * half + source_col % half

        @pl.when((source_col // half) == front)
        def _():
            send(off, recv_ref.at[0, where, part]).wait_recv()

        send(off, stage_ref.at[slot]).wait_send()
        return carry

    lax.fori_loop(1, peers, finish, 0)

    @pl.when(kept)
    def _():
        own.wait()

    def close(where, carry):
        forward(stage_ref.at[where], where).wait_send()
        forward(stage_ref.at[where], where).wait_recv()
        return carry

    lax.fori_loop(0, row_count * half, close, 0)


def exchange(outgoing, prior, diagonal, tokens, sizes, low, count, number):
    row_count, col_count, half = sizes
    peers = row_count * col_count
    slots = row_count * half
    cap_rows, cap_cols = outgoing.shape[1:3]
    anywhere = pl.BlockSpec(memory_space=pl.ANY)
    vmem = pl.BlockSpec(memory_space=pltpu.VMEM)
    factoring = diagonal is not None
    operands, in_specs = [outgoing], [anywhere]
    if factoring:
        operands.append(diagonal)
        in_specs.append(vmem)
    operands += tokens
    in_specs += [anywhere] * len(tokens)
    aliases = {}
    if prior is not None:
        aliases = {len(operands): 0}
        operands.append(prior)
        in_specs.append(anywhere)
    out_shape = [
        jax.ShapeDtypeStruct((2, slots, cap_rows, cap_cols, TILE, TILE), outgoing.dtype),
        jax.ShapeDtypeStruct((slots, count, cap_cols, TILE, TILE), outgoing.dtype),
    ]
    out_specs = [anywhere, anywhere]
    scratch = []
    if factoring:
        out_shape.append(jax.ShapeDtypeStruct((KW, KW), jnp.float32))
        out_specs.append(vmem)
        scratch = [
            pltpu.VMEM((KW, 2 * KW), jnp.float32),
            pltpu.VMEM((TILE, 2 * TILE), jnp.float32),
        ]
    sent = peers * count * cap_cols * TILE * TILE * 2
    return pl.pallas_call(
        functools.partial(exchange_kernel, sizes, low, count, len(operands), factoring),
        out_shape=out_shape,
        in_specs=in_specs,
        out_specs=out_specs,
        scratch_shapes=scratch
        + [
            pltpu.SemaphoreType.DMA((peers,)),
            pltpu.SemaphoreType.DMA((peers,)),
            pltpu.SemaphoreType.DMA((slots,)),
            pltpu.SemaphoreType.DMA((slots,)),
            pltpu.SemaphoreType.DMA,
        ],
        input_output_aliases=aliases,
        compiler_params=pltpu.CompilerParams(
            collective_id=number, has_side_effects=True, vmem_limit_bytes=56 * 2**20
        ),
        cost_estimate=pl.CostEstimate(flops=0, bytes_accessed=70 * sent, transcendentals=0),
        name="exchange_tiles_%d" % number,
    )(*operands)


def combine_kernel(row_count, rows_at, local_ct, cap_cols, update, place_ref, cols_ref, *refs):
    step = pl.program_id(0)
    tiles = refs[: 2 * rows_at]
    front_ref = refs[2 * rows_at]
    out_ref = refs[-2] if update else refs[-1]
    for at in range(rows_at):
        span = pl.ds(at * TILE, TILE)
        for ct in range(local_ct):
            lanes = pl.ds(ct * TILE, TILE)
            total = front_ref[0, span, lanes].astype(jnp.float32)
            for sib in range(2):
                where = cols_ref[sib, ct]
                there = (place_ref[3, sib, step * rows_at + at] > 0) & (where >= 0)
                where = jnp.maximum(where, 0)
                tile = tiles[2 * at + sib][0, where // cap_cols, 0, where % cap_cols]
                total = total + jnp.where(there, tile.astype(jnp.float32), 0.0)
            out_ref[0, span, lanes] = total
    if update:
        right_ref = refs[2 * rows_at + 1]
        shares = refs[2 * rows_at + 2 : 3 * rows_at + 2]
        factor_ref = refs[-1]
        lefts = []
        panel_of = lax.broadcasted_iota(jnp.int32, (TILE, KW), 1) // PANEL
        for at in range(rows_at):
            values = shares[at][0, 0]
            factor_ref[0, pl.ds(at * TILE, TILE), :] = values
            tile_no = lax.axis_index("row") + row_count * (step * rows_at + at)
            lefts.append(
                jnp.where(tile_no >= 2 * panel_of + 2, values, 0.0).astype(jnp.bfloat16)
            )
        left = jnp.concatenate(lefts, axis=0)
        for ct in range(0, local_ct, 2):
            lanes = pl.ds(ct * TILE, 2 * TILE)
            out_ref[0, :, lanes] -= lax.dot_general(
                left, right_ref[:, lanes], (((1,), (0,)), ((), ())),
                preferred_element_type=jnp.float32,
            )


def combine(recv, front_block, place, cols, sizes, row_tiles, rows_at, factors):
    row_count, col_count, half = sizes
    quarter = half // 2
    cap_rows, cap_cols = recv.shape[2:4]
    width = front_block.shape[2]
    local_ct = width // TILE

    recv = recv.reshape(2, row_count * 2, quarter, cap_rows, cap_cols, TILE, TILE)
    recv = recv.reshape(4 * row_count, quarter, cap_rows, cap_cols, TILE, TILE)

    def block_map(at, sib, step, place_ref, cols_ref):
        tile = step * rows_at + at
        return (place_ref[0, sib, tile], 0, place_ref[1, sib, tile], 0, 0, 0)

    in_specs = []
    for at in range(rows_at):
        for sib in range(2):
            in_specs.append(
                pl.BlockSpec(
                    (1, quarter, 1, cap_cols, TILE, TILE), functools.partial(block_map, at, sib)
                )
            )
    in_specs.append(pl.BlockSpec((1, rows_at * TILE, width), lambda step, *_: (0, step, 0)))
    operands = [recv] * (2 * rows_at) + [front_block]
    if factors is not None:
        right, shares = factors
        ratio = col_count // row_count

        def share_map(at, step, *_):
            tile = step * rows_at + at
            return (tile % ratio, tile // ratio, 0, 0)

        in_specs.append(pl.BlockSpec((KW, width), lambda step, *_: (0, 0)))
        for at in range(rows_at):
            in_specs.append(pl.BlockSpec((1, 1, TILE, KW), functools.partial(share_map, at)))
        operands += [right] + [shares] * rows_at
    row_block = lambda step, *_: (0, step, 0)
    out_shape = jax.ShapeDtypeStruct((1, row_tiles * TILE, width), jnp.float32)
    out_specs = pl.BlockSpec((1, rows_at * TILE, width), row_block)
    if factors is not None:
        out_shape = (out_shape, jax.ShapeDtypeStruct((1, row_tiles * TILE, KW), jnp.float32))
        out_specs = (out_specs, pl.BlockSpec((1, rows_at * TILE, KW), row_block))
    return pl.pallas_call(
        functools.partial(combine_kernel, row_count, rows_at, local_ct, cap_cols, factors is not None),
        grid_spec=pltpu.PrefetchScalarGridSpec(
            num_scalar_prefetch=2,
            grid=(row_tiles // rows_at,),
            in_specs=in_specs,
            out_specs=out_specs,
        ),
        out_shape=out_shape,
        compiler_params=pltpu.CompilerParams(vmem_limit_bytes=54 * 2**20),
        name="combine_update" if factors is not None else "combine_pivot_rows",
    )(place, cols, *operands)


def per_device(front_orig, child_update, tile_map):
    row_count = lax.axis_size("row")
    col_count = lax.axis_size("col")
    front_id = lax.axis_index("front")
    row_id = lax.axis_index("row")
    col_id = lax.axis_index("col")
    local_rt = front_orig.shape[1] // TILE
    local_ct = front_orig.shape[2] // TILE
    band_rows = child_update.shape[0] // TILE
    band_cols = child_update.shape[1] // TILE
    nct = tile_map.shape[2]
    cap_rows = max(1, band_rows // row_count)
    cap_cols = max(1, band_cols // col_count)
    half = col_count // 2
    quarter = col_count // 4
    ratio = col_count // row_count
    sizes = (row_count, col_count, half)
    pivot_tiles = max(1, KT // row_count)

    every = jnp.arange(nct)
    band_of = every // band_rows
    same = (band_of[:, None] == band_of[None, :]) & (
        tile_map[..., :, None] % row_count == tile_map[..., None, :] % row_count
    )
    before = same & (tile_map[..., None, :] < tile_map[..., :, None])
    rank = jnp.sum(before.astype(jnp.int32), axis=-1)

    child_no = col_id // quarter
    sender_map = tile_map[child_no // 2, child_no % 2]
    sender_rank = rank[child_no // 2, child_no % 2]
    first = (front_id * row_count + row_id) * band_rows
    band_map = lax.dynamic_slice(sender_map, (first,), (band_rows,))
    band_rank = lax.dynamic_slice(sender_rank, (first,), (band_rows,))
    wanted = jnp.arange(row_count * cap_rows)[:, None]
    rows = jnp.sum(
        jnp.where(
            (band_map % row_count * cap_rows + band_rank)[None, :] == wanted,
            jnp.arange(band_rows)[None, :],
            0,
        ),
        axis=1,
    ).reshape(row_count, cap_rows)
    col_map = lax.dynamic_slice(sender_map, (col_id % quarter * band_cols,), (band_cols,))
    wanted = jnp.arange(col_count * cap_cols)[:, None]
    cols = jnp.sum(
        jnp.where(
            (col_map % col_count * cap_cols + jnp.arange(band_cols) // col_count)[None, :]
            == wanted,
            jnp.arange(band_cols)[None, :],
            0,
        ),
        axis=1,
    )
    outgoing = pack(
        child_update, rows.astype(jnp.int32), cols.astype(jnp.int32),
        row_count, col_count, cap_rows, cap_cols,
    )

    own_maps = lax.dynamic_index_in_dim(tile_map, front_id, 0, keepdims=False)
    own_rank = lax.dynamic_index_in_dim(rank, front_id, 0, keepdims=False)
    row_tile = row_id + row_count * jnp.arange(local_rt)
    hit = own_maps[:, None, :] == row_tile[None, :, None]
    source = (every // band_rows)[None, None, :]
    side = jnp.where(source // row_count == front_id, 0, 1)
    sib_no = jnp.arange(2)[:, None, None]
    chunk = (side * row_count + source % row_count) * 2 + sib_no

    def choose(values):
        return jnp.sum(jnp.where(hit, values, 0), axis=-1)

    place = jnp.stack(
        [
            choose(chunk),
            choose(own_rank[:, None, :]),
            jnp.zeros((2, local_rt), jnp.int32),
            choose(1),
        ]
    ).astype(jnp.int32)
    col_tile = col_id + col_count * jnp.arange(local_ct)
    col_hit = own_maps[:, None, :] == col_tile[None, :, None]
    col_place = every // band_cols * cap_cols + every % band_cols // col_count
    col_where = jnp.sum(jnp.where(col_hit, col_place + 1, 0), axis=-1).astype(jnp.int32) - 1

    early = min(pivot_tiles, cap_rows)
    bulk = cap_rows - early
    cuts = [early + bulk * at // 3 for at in range(4)]
    recv = exchange(outgoing, None, None, [], sizes, 0, early, 1)[0]
    pivot_rows = combine(
        recv, front_orig, place, col_where, sizes, pivot_tiles, 1, None
    )[0]
    gathered = lax.all_gather(pivot_rows.reshape(pivot_tiles, TILE, -1), "row", axis=0)
    gathered = gathered.swapaxes(0, 1).reshape(row_count * pivot_tiles * TILE, -1)[:KW]
    corner = pivot_rows[:, :TILE].reshape(pivot_tiles, TILE, TILE)
    corner = lax.all_gather(corner, ("row", "col"), axis=0)
    corner = corner.reshape(row_count, col_count, pivot_tiles, TILE, TILE)[:, :KT]
    diagonal = corner.transpose(2, 0, 3, 1, 4).reshape(-1, KW)[:KW]

    if bulk >= 3:
        recv = exchange(
            outgoing, recv, None, [pivot_rows], sizes, cuts[0], cuts[1] - cuts[0], 2
        )[0]
        recv, _, inverse = exchange(
            outgoing, recv, diagonal, [], sizes, cuts[1], cuts[2] - cuts[1], 3
        )
    else:
        inverse = factor_alone(diagonal)

    col_tiles = jnp.repeat(col_tile, TILE)[None, :]
    mine = lax.dot_general(
        inverse, gathered, (((1,), (0,)), ((), ())),
        precision=HI, preferred_element_type=jnp.float32,
    )
    panel_of = jnp.arange(KW)[:, None] // PANEL
    mine = jnp.where(col_tiles >= 2 * panel_of, mine, 0.0)
    right = jnp.where(col_tiles >= 2 * panel_of + 2, mine, 0.0).astype(jnp.bfloat16)

    groups = [[q * row_count + h for h in range(row_count)] for q in range(ratio)]
    share = mine.T.reshape(row_count, local_ct * TILE // row_count, KW)
    share = lax.all_to_all(
        share, "col", split_axis=0, concat_axis=0, axis_index_groups=groups, tiled=True
    )
    share = lax.dynamic_index_in_dim(share, row_id, 0, keepdims=False)
    whole = lax.all_gather(share, "col", axis=0)
    if bulk >= 3:
        recv = exchange(
            outgoing, recv, None, [share], sizes, cuts[2], cuts[3] - cuts[2], 4
        )[0]
    elif bulk:
        recv = exchange(outgoing, recv, None, [share], sizes, early, bulk, 5)[0]
    return combine(
        recv, front_orig, place, col_where, sizes, local_rt, 2,
        (right, whole.reshape(ratio, local_ct, TILE, KW)),
    )


def solution(mesh):
    placed = (P("front", "row", "col"), P(("front", "row"), "col"), P())
    return jax.shard_map(
        per_device,
        mesh=mesh,
        in_specs=placed,
        out_specs=(P("front", "row", "col"), P("front", "row", None)),
        check_vma=False,
    )
```

```python
import functools

import jax
import jax.numpy as jnp
from jax import lax
from jax.experimental import pallas as pl
from jax.experimental.pallas import tpu as pltpu
from jax.sharding import PartitionSpec as P

TILE = 128
PANELS = 2
PANEL = 256
KT = PANELS * PANEL // TILE
KW = KT * TILE
HI = lax.Precision.HIGHEST
MESH = pl.DeviceIdType.MESH


def pack(child, rows, cols, row_count, col_count, cap_rows, cap_cols):
    peers = row_count * col_count
    width = child.shape[1]

    def body(rows_ref, cols_ref, *refs):
        ins, out_ref = refs[:-1], refs[-1]
        for dest_row in range(row_count):
            for dest_col in range(col_count):
                for slot in range(cap_cols):
                    col = pl.multiple_of(cols_ref[dest_col * cap_cols + slot] * TILE, TILE)
                    out_ref[dest_row * col_count + dest_col, 0, slot] = ins[dest_row][
                        :, pl.ds(col, TILE)
                    ]

    def row_map(dest_row, step, rows_ref, cols_ref):
        return (rows_ref[dest_row, step], 0)

    return pl.pallas_call(
        body,
        grid_spec=pltpu.PrefetchScalarGridSpec(
            num_scalar_prefetch=2,
            grid=(cap_rows,),
            in_specs=[
                pl.BlockSpec((TILE, width), functools.partial(row_map, dest_row))
                for dest_row in range(row_count)
            ],
            out_specs=pl.BlockSpec(
                (peers, 1, cap_cols, TILE, TILE), lambda step, *_: (0, step, 0, 0, 0)
            ),
        ),
        out_shape=jax.ShapeDtypeStruct((peers, cap_rows, cap_cols, TILE, TILE), child.dtype),
        compiler_params=pltpu.CompilerParams(vmem_limit_bytes=40 * 2**20),
        name="pack_tiles",
    )(rows, cols, *([child] * row_count))


def invert_factor(diag_ref, inv_ref, work_ref, small_ref, between):
    blocks = KW // TILE
    rows_of = lax.broadcasted_iota(jnp.int32, (KW, KW), 0)
    cols_of = lax.broadcasted_iota(jnp.int32, (KW, KW), 1)
    work_ref[:, :KW] = diag_ref[...]
    work_ref[:, KW:] = jnp.where(rows_of == cols_of, 1.0, 0.0)
    row_no = lax.broadcasted_iota(jnp.int32, (TILE, 1), 0)
    lane_no = lax.broadcasted_iota(jnp.int32, (1, TILE), 1)
    small_rows = lax.broadcasted_iota(jnp.int32, (TILE, TILE), 0)
    small_cols = lax.broadcasted_iota(jnp.int32, (TILE, TILE), 1)
    for block in range(blocks):
        span = pl.ds(block * TILE, TILE)
        small_ref[:, :TILE] = work_ref[span, span]
        small_ref[:, TILE:] = jnp.where(small_rows == small_cols, 1.0, 0.0)

        def step(k, carry):
            pivot_row = small_ref[pl.ds(k, 1), :]
            here = lane_no == k
            pivot = jnp.sum(jnp.where(here, pivot_row[:, :TILE], 0.0), axis=1, keepdims=True)
            scale = 1.0 / jnp.sqrt(pivot)
            column = jnp.sum(jnp.where(here, small_ref[:, :TILE], 0.0), axis=1, keepdims=True)
            scaled = pivot_row * scale
            times = jnp.where(row_no > k, column * scale, 0.0)
            small_ref[...] = jnp.where(row_no == k, scaled, small_ref[...] - times * scaled)
            return carry

        lax.fori_loop(0, TILE, step, 0)
        reduced = jnp.dot(
            small_ref[:, TILE:], work_ref[span, :], precision=HI,
            preferred_element_type=jnp.float32,
        )
        work_ref[span, :] = reduced
        if block + 1 < blocks:
            rest = pl.ds((block + 1) * TILE, KW - (block + 1) * TILE)
            work_ref[rest, :] -= lax.dot_general(
                work_ref[span, rest], work_ref[span, :], (((0,), (0,)), ((), ())),
                precision=HI, preferred_element_type=jnp.float32,
            )
        between(block)
    inv_ref[...] = jnp.where(rows_of >= cols_of, work_ref[:, KW:], 0.0)


def factor_alone(diagonal):
    def body(diag_ref, inv_ref, work_ref, small_ref):
        invert_factor(diag_ref, inv_ref, work_ref, small_ref, lambda block: None)

    return pl.pallas_call(
        body,
        out_shape=jax.ShapeDtypeStruct((KW, KW), jnp.float32),
        scratch_shapes=[
            pltpu.VMEM((KW, 2 * KW), jnp.float32),
            pltpu.VMEM((TILE, 2 * TILE), jnp.float32),
        ],
        compiler_params=pltpu.CompilerParams(vmem_limit_bytes=32 * 2**20),
        name="factor_inverse",
    )(diagonal)


def exchange_kernel(sizes, low, count, inputs, factoring, *refs):
    row_count, col_count, half = sizes
    out_ref = refs[0]
    recv_ref, stage_ref = refs[inputs : inputs + 2]
    if factoring:
        inv_ref, work_ref, small_ref = refs[inputs + 2], refs[-7], refs[-6]
    send_sem, recv_sem, pass_send, pass_recv, own_sem = refs[-5:]
    peers = row_count * col_count
    front = lax.axis_index("front")
    row = lax.axis_index("row")
    col = lax.axis_index("col")
    me = row * col_count + col
    kept = (col // half) == front
    slot = row * half + col % half
    part = pl.ds(low, count)

    barrier = pltpu.get_barrier_semaphore()

    def greet(off, carry):
        dest = (me + off) % peers
        pl.semaphore_signal(
            barrier, inc=1, device_id=(front, dest // col_count, dest % col_count),
            device_id_type=MESH,
        )
        return carry

    lax.fori_loop(1, peers, greet, 0)
    pl.semaphore_signal(barrier, inc=1, device_id=(1 - front, row, col), device_id_type=MESH)
    pl.semaphore_wait(barrier, peers)

    def send(off, target):
        dest = (me + off) % peers
        return pltpu.make_async_remote_copy(
            src_ref=out_ref.at[dest, part],
            dst_ref=target,
            send_sem=send_sem.at[off],
            recv_sem=recv_sem.at[off],
            device_id=(front, dest // col_count, dest % col_count),
            device_id_type=MESH,
        )

    def forward(source, where):
        return pltpu.make_async_remote_copy(
            src_ref=source,
            dst_ref=recv_ref.at[1, where, part],
            send_sem=pass_send.at[where],
            recv_sem=pass_recv.at[where],
            device_id=(1 - front, row, col),
            device_id_type=MESH,
        )

    own = pltpu.make_async_copy(out_ref.at[me, part], recv_ref.at[0, slot, part], own_sem)

    @pl.when(kept)
    def _():
        def start(off, carry):
            send(off, recv_ref.at[0, slot, part]).start()
            return carry

        lax.fori_loop(1, peers, start, 0)
        own.start()

    @pl.when(jnp.logical_not(kept))
    def _():
        def start(off, carry):
            send(off, stage_ref.at[slot]).start()
            return carry

        lax.fori_loop(1, peers, start, 0)
        forward(out_ref.at[me, part], slot).start()

    def relay(off, carry):
        source = (me + peers - off) % peers
        source_col = source % col_count
        where = (source // col_count) * half + source_col % half

        @pl.when((source_col // half) != front)
        def _():
            send(off, stage_ref.at[where]).wait_recv()
            forward(stage_ref.at[where], where).start()

        return carry

    if factoring:
        parts = KW // TILE
        cuts = [1 + (peers - 1) * at // parts for at in range(parts + 1)]

        def between(block):
            lax.fori_loop(cuts[block], cuts[block + 1], relay, 0)

        invert_factor(refs[1], inv_ref, work_ref, small_ref, between)
    else:
        lax.fori_loop(1, peers, relay, 0)

    def finish(off, carry):
        source = (me + peers - off) % peers
        source_col = source % col_count
        where = (source // col_count) * half + source_col % half

        @pl.when((source_col // half) == front)
        def _():
            send(off, recv_ref.at[0, where, part]).wait_recv()

        send(off, stage_ref.at[slot]).wait_send()
        return carry

    lax.fori_loop(1, peers, finish, 0)

    @pl.when(kept)
    def _():
        own.wait()

    def close(where, carry):
        forward(stage_ref.at[where], where).wait_send()
        forward(stage_ref.at[where], where).wait_recv()
        return carry

    lax.fori_loop(0, row_count * half, close, 0)


def exchange(outgoing, prior, diagonal, tokens, sizes, low, count, number):
    row_count, col_count, half = sizes
    peers = row_count * col_count
    slots = row_count * half
    cap_rows, cap_cols = outgoing.shape[1:3]
    anywhere = pl.BlockSpec(memory_space=pl.ANY)
    vmem = pl.BlockSpec(memory_space=pltpu.VMEM)
    factoring = diagonal is not None
    operands, in_specs = [outgoing], [anywhere]
    if factoring:
        operands.append(diagonal)
        in_specs.append(vmem)
    operands += tokens
    in_specs += [anywhere] * len(tokens)
    aliases = {}
    if prior is not None:
        aliases = {len(operands): 0}
        operands.append(prior)
        in_specs.append(anywhere)
    out_shape = [
        jax.ShapeDtypeStruct((2, slots, cap_rows, cap_cols, TILE, TILE), outgoing.dtype),
        jax.ShapeDtypeStruct((slots, count, cap_cols, TILE, TILE), outgoing.dtype),
    ]
    out_specs = [anywhere, anywhere]
    scratch = []
    if factoring:
        out_shape.append(jax.ShapeDtypeStruct((KW, KW), jnp.float32))
        out_specs.append(vmem)
        scratch = [
            pltpu.VMEM((KW, 2 * KW), jnp.float32),
            pltpu.VMEM((TILE, 2 * TILE), jnp.float32),
        ]
    sent = peers * count * cap_cols * TILE * TILE * 2
    return pl.pallas_call(
        functools.partial(exchange_kernel, sizes, low, count, len(operands), factoring),
        out_shape=out_shape,
        in_specs=in_specs,
        out_specs=out_specs,
        scratch_shapes=scratch
        + [
            pltpu.SemaphoreType.DMA((peers,)),
            pltpu.SemaphoreType.DMA((peers,)),
            pltpu.SemaphoreType.DMA((slots,)),
            pltpu.SemaphoreType.DMA((slots,)),
            pltpu.SemaphoreType.DMA,
        ],
        input_output_aliases=aliases,
        compiler_params=pltpu.CompilerParams(
            collective_id=number, has_side_effects=True, vmem_limit_bytes=56 * 2**20
        ),
        cost_estimate=pl.CostEstimate(flops=0, bytes_accessed=70 * sent, transcendentals=0),
        name="exchange_tiles_%d" % number,
    )(*operands)


def combine_kernel(row_count, rows_at, local_ct, cap_cols, update, place_ref, cols_ref, *refs):
    step = pl.program_id(0)
    tiles = refs[: 2 * rows_at]
    front_ref = refs[2 * rows_at]
    out_ref = refs[-2] if update else refs[-1]
    for at in range(rows_at):
        span = pl.ds(at * TILE, TILE)
        for ct in range(local_ct):
            lanes = pl.ds(ct * TILE, TILE)
            total = front_ref[0, span, lanes].astype(jnp.float32)
            for sib in range(2):
                where = cols_ref[sib, ct]
                there = (place_ref[3, sib, step * rows_at + at] > 0) & (where >= 0)
                where = jnp.maximum(where, 0)
                tile = tiles[2 * at + sib][0, where // cap_cols, 0, where % cap_cols]
                total = total + jnp.where(there, tile.astype(jnp.float32), 0.0)
            out_ref[0, span, lanes] = total
    if update:
        right_ref = refs[2 * rows_at + 1]
        shares = refs[2 * rows_at + 2 : 3 * rows_at + 2]
        factor_ref = refs[-1]
        lefts = []
        panel_of = lax.broadcasted_iota(jnp.int32, (TILE, KW), 1) // PANEL
        for at in range(rows_at):
            values = shares[at][0, 0]
            factor_ref[0, pl.ds(at * TILE, TILE), :] = values
            tile_no = lax.axis_index("row") + row_count * (step * rows_at + at)
            lefts.append(
                jnp.where(tile_no >= 2 * panel_of + 2, values, 0.0).astype(jnp.bfloat16)
            )
        left = jnp.concatenate(lefts, axis=0)
        for ct in range(0, local_ct, 2):
            lanes = pl.ds(ct * TILE, 2 * TILE)
            out_ref[0, :, lanes] -= lax.dot_general(
                left, right_ref[:, lanes], (((1,), (0,)), ((), ())),
                preferred_element_type=jnp.float32,
            )


def combine(recv, front_block, place, cols, sizes, row_tiles, rows_at, factors):
    row_count, col_count, half = sizes
    quarter = half // 2
    cap_rows, cap_cols = recv.shape[2:4]
    width = front_block.shape[2]
    local_ct = width // TILE

    recv = recv.reshape(2, row_count * 2, quarter, cap_rows, cap_cols, TILE, TILE)
    recv = recv.reshape(4 * row_count, quarter, cap_rows, cap_cols, TILE, TILE)

    def block_map(at, sib, step, place_ref, cols_ref):
        tile = step * rows_at + at
        return (place_ref[0, sib, tile], 0, place_ref[1, sib, tile], 0, 0, 0)

    in_specs = []
    for at in range(rows_at):
        for sib in range(2):
            in_specs.append(
                pl.BlockSpec(
                    (1, quarter, 1, cap_cols, TILE, TILE), functools.partial(block_map, at, sib)
                )
            )
    in_specs.append(pl.BlockSpec((1, rows_at * TILE, width), lambda step, *_: (0, step, 0)))
    operands = [recv] * (2 * rows_at) + [front_block]
    if factors is not None:
        right, shares = factors
        ratio = col_count // row_count

        def share_map(at, step, *_):
            tile = step * rows_at + at
            return (tile % ratio, tile // ratio, 0, 0)

        in_specs.append(pl.BlockSpec((KW, width), lambda step, *_: (0, 0)))
        for at in range(rows_at):
            in_specs.append(pl.BlockSpec((1, 1, TILE, KW), functools.partial(share_map, at)))
        operands += [right] + [shares] * rows_at
    row_block = lambda step, *_: (0, step, 0)
    out_shape = jax.ShapeDtypeStruct((1, row_tiles * TILE, width), jnp.float32)
    out_specs = pl.BlockSpec((1, rows_at * TILE, width), row_block)
    if factors is not None:
        out_shape = (out_shape, jax.ShapeDtypeStruct((1, row_tiles * TILE, KW), jnp.float32))
        out_specs = (out_specs, pl.BlockSpec((1, rows_at * TILE, KW), row_block))
    return pl.pallas_call(
        functools.partial(combine_kernel, row_count, rows_at, local_ct, cap_cols, factors is not None),
        grid_spec=pltpu.PrefetchScalarGridSpec(
            num_scalar_prefetch=2,
            grid=(row_tiles // rows_at,),
            in_specs=in_specs,
            out_specs=out_specs,
        ),
        out_shape=out_shape,
        compiler_params=pltpu.CompilerParams(vmem_limit_bytes=54 * 2**20),
        name="combine_update" if factors is not None else "combine_pivot_rows",
    )(place, cols, *operands)


def per_device(front_orig, child_update, tile_map):
    row_count = lax.axis_size("row")
    col_count = lax.axis_size("col")
    front_id = lax.axis_index("front")
    row_id = lax.axis_index("row")
    col_id = lax.axis_index("col")
    local_rt = front_orig.shape[1] // TILE
    local_ct = front_orig.shape[2] // TILE
    band_rows = child_update.shape[0] // TILE
    band_cols = child_update.shape[1] // TILE
    nct = tile_map.shape[2]
    cap_rows = max(1, band_rows // row_count)
    cap_cols = max(1, band_cols // col_count)
    half = col_count // 2
    quarter = col_count // 4
    ratio = col_count // row_count
    sizes = (row_count, col_count, half)
    pivot_tiles = max(1, KT // row_count)

    every = jnp.arange(nct)
    band_of = every // band_rows
    same = (band_of[:, None] == band_of[None, :]) & (
        tile_map[..., :, None] % row_count == tile_map[..., None, :] % row_count
    )
    before = same & (tile_map[..., None, :] < tile_map[..., :, None])
    rank = jnp.sum(before.astype(jnp.int32), axis=-1)

    child_no = col_id // quarter
    sender_map = tile_map[child_no // 2, child_no % 2]
    sender_rank = rank[child_no // 2, child_no % 2]
    first = (front_id * row_count + row_id) * band_rows
    band_map = lax.dynamic_slice(sender_map, (first,), (band_rows,))
    band_rank = lax.dynamic_slice(sender_rank, (first,), (band_rows,))
    wanted = jnp.arange(row_count * cap_rows)[:, None]
    rows = jnp.sum(
        jnp.where(
            (band_map % row_count * cap_rows + band_rank)[None, :] == wanted,
            jnp.arange(band_rows)[None, :],
            0,
        ),
        axis=1,
    ).reshape(row_count, cap_rows)
    col_map = lax.dynamic_slice(sender_map, (col_id % quarter * band_cols,), (band_cols,))
    wanted = jnp.arange(col_count * cap_cols)[:, None]
    cols = jnp.sum(
        jnp.where(
            (col_map % col_count * cap_cols + jnp.arange(band_cols) // col_count)[None, :]
            == wanted,
            jnp.arange(band_cols)[None, :],
            0,
        ),
        axis=1,
    )
    outgoing = pack(
        child_update, rows.astype(jnp.int32), cols.astype(jnp.int32),
        row_count, col_count, cap_rows, cap_cols,
    )

    own_maps = lax.dynamic_index_in_dim(tile_map, front_id, 0, keepdims=False)
    own_rank = lax.dynamic_index_in_dim(rank, front_id, 0, keepdims=False)
    row_tile = row_id + row_count * jnp.arange(local_rt)
    hit = own_maps[:, None, :] == row_tile[None, :, None]
    source = (every // band_rows)[None, None, :]
    side = jnp.where(source // row_count == front_id, 0, 1)
    sib_no = jnp.arange(2)[:, None, None]
    chunk = (side * row_count + source % row_count) * 2 + sib_no

    def choose(values):
        return jnp.sum(jnp.where(hit, values, 0), axis=-1)

    place = jnp.stack(
        [
            choose(chunk),
            choose(own_rank[:, None, :]),
            jnp.zeros((2, local_rt), jnp.int32),
            choose(1),
        ]
    ).astype(jnp.int32)
    col_tile = col_id + col_count * jnp.arange(local_ct)
    col_hit = own_maps[:, None, :] == col_tile[None, :, None]
    col_place = every // band_cols * cap_cols + every % band_cols // col_count
    col_where = jnp.sum(jnp.where(col_hit, col_place + 1, 0), axis=-1).astype(jnp.int32) - 1

    early = min(pivot_tiles, cap_rows)
    bulk = cap_rows - early
    cuts = [early, early + bulk // 3, cap_rows - max(1, bulk // 6), cap_rows]
    recv = exchange(outgoing, None, None, [], sizes, 0, early, 1)[0]
    pivot_rows = combine(
        recv, front_orig, place, col_where, sizes, pivot_tiles, 1, None
    )[0]
    gathered = lax.all_gather(pivot_rows.reshape(pivot_tiles, TILE, -1), "row", axis=0)
    gathered = gathered.swapaxes(0, 1).reshape(row_count * pivot_tiles * TILE, -1)[:KW]
    corner = pivot_rows[:, :TILE].reshape(pivot_tiles, TILE, TILE)
    corner = lax.all_gather(corner, ("row", "col"), axis=0)
    corner = corner.reshape(row_count, col_count, pivot_tiles, TILE, TILE)[:, :KT]
    diagonal = corner.transpose(2, 0, 3, 1, 4).reshape(-1, KW)[:KW]

    if bulk >= 3:
        recv = exchange(
            outgoing, recv, None, [pivot_rows], sizes, cuts[0], cuts[1] - cuts[0], 2
        )[0]
        recv, _, inverse = exchange(
            outgoing, recv, diagonal, [], sizes, cuts[1], cuts[2] - cuts[1], 3
        )
    else:
        inverse = factor_alone(diagonal)

    col_tiles = jnp.repeat(col_tile, TILE)[None, :]
    mine = lax.dot_general(
        inverse, gathered, (((1,), (0,)), ((), ())),
        precision=HI, preferred_element_type=jnp.float32,
    )
    panel_of = jnp.arange(KW)[:, None] // PANEL
    mine = jnp.where(col_tiles >= 2 * panel_of, mine, 0.0)
    right = jnp.where(col_tiles >= 2 * panel_of + 2, mine, 0.0).astype(jnp.bfloat16)

    groups = [[q * row_count + h for h in range(row_count)] for q in range(ratio)]
    share = mine.T.reshape(row_count, local_ct * TILE // row_count, KW)
    share = lax.all_to_all(
        share, "col", split_axis=0, concat_axis=0, axis_index_groups=groups, tiled=True
    )
    share = lax.dynamic_index_in_dim(share, row_id, 0, keepdims=False)
    whole = lax.all_gather(share, "col", axis=0)
    if bulk >= 3:
        recv = exchange(
            outgoing, recv, None, [share], sizes, cuts[2], cuts[3] - cuts[2], 4
        )[0]
    elif bulk:
        recv = exchange(outgoing, recv, None, [share], sizes, early, bulk, 5)[0]
    return combine(
        recv, front_orig, place, col_where, sizes, local_rt, 4,
        (right, whole.reshape(ratio, local_ct, TILE, KW)),
    )


def solution(mesh):
    placed = (P("front", "row", "col"), P(("front", "row"), "col"), P())
    return jax.shard_map(
        per_device,
        mesh=mesh,
        in_specs=placed,
        out_specs=(P("front", "row", "col"), P("front", "row", None)),
        check_vma=False,
    )
```
